256 devices in a mesh: section: 2 (over z_lo), dp: 8 (over z_hi, core), tensor: 16 (over x, y).
Axes of the slice: x: 4, y: 4, z: 8 (z_hi: 4, z_lo: 2; z = z_hi * 2 + z_lo), core: 2. Of those that a mesh axis runs over, the one named last changes fastest.
Arguments:
- tokens: bfloat16 [4, 128, 8192], P(None, None, 'dp'), may hold values from -6 to 6
- w_in: bfloat16 [2, 8192, 14336], P('section', 'dp', 'tensor'), may hold values from -2 to 2
- w_out: bfloat16 [2, 14336, 8192], P('section', 'tensor', 'dp'), may hold values from -0.046875 to 0.046875
- cotangent: bfloat16 [4, 128, 8192], P(None, None, 'dp'), may hold values from -6 to 6
Outputs:
- section_out: bfloat16 [2, 4, 128, 8192], P('section', None, None, 'dp')
- input_grad: bfloat16 [2, 4, 128, 8192], P('section', None, None, 'dp')
- w_in_grad: bfloat16 [2, 8192, 14336], P('section', 'dp', 'tensor')
- w_out_grad: bfloat16 [2, 14336, 8192], P('section', 'tensor', 'dp')
The draws below stay inside these ranges and needn't reach their ends.
All inputs are finite; a program needn't handle non-finite values.
Results may differ from the reference program's by a relative error of at most 0.013.
The reference program's roundings to bfloat16 on the way (of `normed_bf`, `hidden` and `grad_pre`) count: a program that leaves them out, or rounds other values in their place, can miss the bound.
Values may be sent and summed in bfloat16 or wider, within the bound.
No kernel may reach another device: no remote copies, remote signals or barrier semaphores. Data moves between devices by JAX's collectives and lax.ppermute only.
A program may use at most 128 MiB of HBM per device.

```python
import math
import jax
import jax.numpy as jnp
from jax import lax

D = 8192
FF = 14336
ROWS = 128
MICRO = 4


def width_profile(key, rise):
    place = jnp.arange(D, dtype=jnp.float32) / D
    rough = jax.random.uniform(key, (2, D, 1), jnp.float32, 0.6, 1.4)
    mean_level = (rise - 1.0) / math.log(rise)
    return jnp.exp(math.log(rise) * place)[None, :, None] * rough / mean_level


def draw_w_in(key, part):
    key = jax.random.fold_in(key, 11)
    key_own, key_level, key_common = jax.random.split(key, 3)
    own = jnp.clip(jax.random.normal(key_own, (2, D, FF), jnp.float32), -4.0, 4.0)
    level = width_profile(key_level, 5.0)
    common = jnp.clip(jax.random.normal(key_common, (2, 1, FF), jnp.float32), -4.0, 4.0)
    values = (own + 0.5 * level * common) / math.sqrt(D)
    return values.astype(jnp.bfloat16)


def block_scale(key, shape, cuts, smallest, top_value):
    loudness = 1.0
    for position, shards_of in cuts:
        steps = jax.random.uniform(jax.random.fold_in(jax.random.fold_in(key, 6), position), (shards_of,), jnp.float32, smallest / len(cuts), top_value / len(cuts))
        loudness = loudness * jnp.repeat(jnp.exp(steps), shape[position] // shards_of).reshape((-1,) + (1,) * (len(shape) - 1 - position))
    return loudness


def scatter_about(stream_key, dims, spread, limit, cuts=(), held_as=jnp.bfloat16):
    result = spread * jax.random.normal(stream_key, dims, jnp.float32)
    if cuts:
        result = result * block_scale(stream_key, dims, cuts, -0.22, 0.18)
    return jnp.clip(result, -limit, limit).astype(held_as)


def setup_inputs(seed: int = 0) -> dict:
    arg_keys = jax.random.split(jax.random.key(seed), 5)
    return {
        "tokens": scatter_about(arg_keys[0], (MICRO, ROWS, D), 1.0, 6.0, ((2, 8),)),
        "w_in": draw_w_in(jax.random.fold_in(arg_keys[4], 71), 0),
        "w_out": scatter_about(arg_keys[2], (2, FF, D), FF ** -0.5, 0.046875, ((0, 2), (1, 16), (2, 8))),
        "cotangent": scatter_about(arg_keys[3], (MICRO, ROWS, D), 1.0, 6.0, ((2, 8),)),
    }


root_two_pi = 0.7978845608

def gelu_value(pre_act):
    inner = jnp.tanh(root_two_pi * (pre_act + 0.044715 * pre_act ** 3))
    return 0.5 * pre_act * (1.0 + inner)

def gelu_slope(pre_act):
    inner = jnp.tanh(root_two_pi * (pre_act + 0.044715 * pre_act ** 3))
    return 0.5 * (1.0 + inner) + 0.5 * pre_act * (1.0 - inner * inner) * root_two_pi * (1.0 + 3.0 * 0.044715 * pre_act * pre_act)

def section_forward(section_input, weight_in, weight_out):
    values = section_input.astype(jnp.float32)
    row_mean = lax.optimization_barrier(jnp.sum(values, 1)) / D
    inv_scale = jax.lax.rsqrt(lax.optimization_barrier(jnp.sum(values * values, 1)) / D - row_mean * row_mean + 1e-05)
    normed = (values - row_mean[:, None]) * inv_scale[:, None]
    normed_bf = normed.astype(jnp.bfloat16)
    pre_act = jnp.dot(normed_bf, weight_in, preferred_element_type=jnp.float32)
    hidden = gelu_value(pre_act).astype(jnp.bfloat16)
    output = (values + jnp.dot(hidden, weight_out, preferred_element_type=jnp.float32)).astype(jnp.bfloat16)
    return (output, normed, normed_bf, inv_scale, pre_act, hidden)

def section_backward(grad_out, saved, weight_in, weight_out):
    output, normed, normed_bf, inv_scale, pre_act, hidden = saved
    grad_hidden = jnp.dot(grad_out, weight_out.T, preferred_element_type=jnp.float32)
    grad_pre = (grad_hidden * gelu_slope(pre_act)).astype(jnp.bfloat16)
    grad_w_out = jnp.dot(hidden.T, grad_out, preferred_element_type=jnp.float32)
    grad_w_in = jnp.dot(normed_bf.T, grad_pre, preferred_element_type=jnp.float32)
    grad_normed = jnp.dot(grad_pre, weight_in.T, preferred_element_type=jnp.float32)
    first_sum = lax.optimization_barrier(jnp.sum(grad_normed, 1)) / D
    second_sum = lax.optimization_barrier(jnp.sum(grad_normed * normed, 1)) / D
    grad_in = (grad_out.astype(jnp.float32) + inv_scale[:, None] * (grad_normed - first_sum[:, None] - normed * second_sum[:, None])).astype(jnp.bfloat16)
    return (grad_in, grad_w_in, grad_w_out)

def reference(tokens, w_in, w_out, cotangent):
    outs_first, outs_second, grads_first, grads_second = ([], [], [], [])
    totals_in = [jnp.zeros(w_in.shape[1:], jnp.float32), jnp.zeros(w_in.shape[1:], jnp.float32)]
    totals_out = [jnp.zeros(w_out.shape[1:], jnp.float32), jnp.zeros(w_out.shape[1:], jnp.float32)]
    for batch_no in range(MICRO):
        saved_first = section_forward(tokens[batch_no], w_in[0], w_out[0])
        saved_second = section_forward(saved_first[0], w_in[1], w_out[1])
        grad_second, gwi_second, gwo_second = section_backward(cotangent[batch_no], saved_second, w_in[1], w_out[1])
        grad_first, gwi_first, gwo_first = section_backward(grad_second, saved_first, w_in[0], w_out[0])
        totals_in[0] = totals_in[0] + gwi_first
        totals_in[1] = totals_in[1] + gwi_second
        totals_out[0] = totals_out[0] + gwo_first
        totals_out[1] = totals_out[1] + gwo_second
        outs_first.append(saved_first[0])
        outs_second.append(saved_second[0])
        grads_first.append(grad_first)
        grads_second.append(grad_second)
    section_out = jnp.stack([jnp.stack(outs_first), jnp.stack(outs_second)])
    input_grad = jnp.stack([jnp.stack(grads_first), jnp.stack(grads_second)])
    w_in_grad = jnp.stack(totals_in).astype(jnp.bfloat16)
    w_out_grad = jnp.stack(totals_out).astype(jnp.bfloat16)
    return (section_out, input_grad, w_in_grad, w_out_grad)
```

```python
import jax
import jax.numpy as jnp
from jax import lax
from jax.sharding import PartitionSpec as P

root_two_pi = 0.7978845608
LANES = 128
EVERYWHERE = ("section", "dp", "tensor")
f32 = jnp.float32
bf16 = jnp.bfloat16


def gelu_value(pre_act):
    inner = jnp.tanh(root_two_pi * (pre_act + 0.044715 * pre_act**3))
    return 0.5 * pre_act * (1.0 + inner)


def gelu_slope(pre_act):
    inner = jnp.tanh(root_two_pi * (pre_act + 0.044715 * pre_act**3))
    return 0.5 * (1.0 + inner) + 0.5 * pre_act * (1.0 - inner * inner) * root_two_pi * (
        1.0 + 3.0 * 0.044715 * pre_act * pre_act
    )


def matmul(a, b):
    return jnp.dot(a, b, preferred_element_type=f32)


def matmul_t(a, b):
    return lax.dot_general(a, b, (((1,), (1,)), ((), ())), preferred_element_type=f32)


def matmul_ta(a, b):
    return lax.dot_general(a, b, (((0,), (0,)), ((), ())), preferred_element_type=f32)


def three_parts(value):
    high = lax.reduce_precision(value, 8, 7)
    rest = value - high
    middle = lax.reduce_precision(rest, 8, 7)
    return high, middle, rest - middle


def pack_side(columns):
    lane = lax.broadcasted_iota(jnp.int32, (1, LANES), 1)
    block = jnp.zeros((columns[0].shape[0], LANES), f32)
    for number, column in enumerate(columns):
        for part_no, part in enumerate(three_parts(column)):
            block = jnp.where(lane == 3 * number + part_no, part, block)
    return block.astype(bf16)


def side_value(block, number):
    lane = lax.broadcasted_iota(jnp.int32, block.shape, block.ndim - 1)
    kept = jnp.where(lane // 3 == number, block.astype(f32), 0.0)
    return jnp.sum(kept, axis=-1, keepdims=True)


def z_route(step, sections, dp_size, tensor_size):
    route = []
    for section in sections:
        for place in range(dp_size):
            other = ((place // 2) ^ step) * 2 + place % 2
            for column in range(tensor_size):
                route.append(
                    (
                        (section * dp_size + place) * tensor_size + column,
                        (section * dp_size + other) * tensor_size + column,
                    )
                )
    return route


def body(tokens, w_in, w_out, cotangent):
    dp_size = lax.axis_size("dp")
    tensor_size = lax.axis_size("tensor")
    z_size = dp_size // 2
    micro, rows_each, own_width = tokens.shape
    rows = micro * rows_each
    half = rows // 2
    z_rows = half // z_size
    t_rows = half // tensor_size
    width = own_width * dp_size
    pair_width = 2 * own_width
    units = w_in.shape[2]
    first_section = lax.axis_index("section") == 0
    place = lax.axis_index("dp")
    z_place, core = place // 2, place % 2
    t_place = lax.axis_index("tensor")

    def pick(early, later):
        return jnp.where(first_section, early, later)

    def core_swap(block):
        return lax.ppermute(block, "dp", [(i, i ^ 1) for i in range(dp_size)])

    def section_hop(block, source):
        return lax.ppermute(block, "section", [(source, 1 - source)])

    def reorder(block):
        parts = block.reshape(2, 2, 2, z_rows, block.shape[1])
        for axis, bit in ((0, core), (1, z_place // 2), (2, z_place % 2)):
            low = lax.index_in_dim(parts, 0, axis)
            high = lax.index_in_dim(parts, 1, axis)
            parts = jnp.concatenate(
                [jnp.where(bit == 1, high, low), jnp.where(bit == 1, low, high)], axis
            )
        return parts.reshape(block.shape)

    def z_blocks(blocks, sections):
        return [blocks[0]] + [
            lax.ppermute(blocks[step], EVERYWHERE, z_route(step, sections, dp_size, tensor_size))
            for step in range(1, z_size)
        ]

    def z_scatter(block, sections):
        return z_blocks([block[k * z_rows : (k + 1) * z_rows] for k in range(z_size)], sections)

    def z_gather(block, sections):
        return jnp.concatenate(z_blocks([block] * z_size, sections), 0)

    def t_scatter(block):
        blocks = block.reshape(tensor_size, t_rows, block.shape[1])
        parts = lax.all_to_all(blocks, "tensor", 0, 0)
        return jnp.sum(parts.astype(f32), 0)

    def t_gather(block):
        copies = jnp.broadcast_to(block[None], (tensor_size,) + block.shape)
        return lax.all_to_all(copies, "tensor", 0, 0)

    def t_slab(block):
        return lax.dynamic_slice_in_dim(block, t_place * t_rows, t_rows, 0)

    def own_columns(block):
        return jnp.concatenate([block[:, :own_width], core_swap(block[:, own_width:])], 0)

    def forward_partial(block):
        values = block.astype(f32)
        total = jnp.sum(values, 1, keepdims=True)
        squares = jnp.sum(values * values, 1, keepdims=True)
        product = matmul(block, w_in_pair) - (total / pair_width) * column_sum
        return jnp.concatenate([product.astype(bf16), pack_side([total, squares])], 1)

    def finish_pre(blocks, sums):
        sides = [block[:, units:] for block in blocks]
        totals = [side_value(side, 0) for side in sides]
        squares = sum(side_value(side, 1) for side in sides)
        mean = sum(totals) / width
        inv_scale = lax.rsqrt(squares / width - mean * mean + 1e-05)
        product = sum(block[:, :units].astype(f32) for block in blocks)
        for total, its_sum in zip(totals, sums):
            product = product + (total / pair_width - mean) * its_sum
        return product * inv_scale, mean, inv_scale

    def backward_sums(grad_pre, pre):
        values = grad_pre.astype(f32)
        first = jnp.sum(values * sum(sums), 1, keepdims=True)
        second = jnp.sum(values * pre, 1, keepdims=True)
        return first, second

    def input_gradient(grad_slab, total, input_slab, side):
        first = side_value(total[:, pair_width:], 2) / width
        second = side_value(total[:, pair_width:], 3) / width
        mean, inv_scale = side_value(t_slab(side), 0), side_value(t_slab(side), 1)
        normed = (input_slab.astype(f32) - mean) * inv_scale
        return (
            grad_slab.astype(f32) + inv_scale * (total[:, :pair_width] - first - normed * second)
        ).astype(bf16)

    with jax.named_scope("tick0"):
        w_in_own, w_out_own = w_in[0], w_out[0]
        w_in_pair = jnp.concatenate([w_in_own, core_swap(w_in_own)], 0)
        w_out_pair = jnp.concatenate([w_out_own, core_swap(w_out_own)], 1)
        in_own = reorder(pick(tokens, cotangent).reshape(rows, own_width))
        in_half = jnp.concatenate([in_own[:half], core_swap(in_own[half:])], 1)
        in_slab = t_slab(in_half)
        column_sum = jnp.sum(w_in_pair.astype(f32), 0, keepdims=True)
        sum_rows = jnp.concatenate(
            list(three_parts(column_sum)) + [jnp.zeros((13, units), f32)], 0
        ).astype(bf16)
        sum_rows = jnp.concatenate([sum_rows, jnp.zeros((16, LANES), bf16)], 1)
        grad_partial = matmul_t(in_half, w_out_pair).astype(bf16)
        grad_partial = jnp.concatenate([grad_partial, jnp.zeros((half, LANES), bf16)], 1)
        partial = pick(forward_partial(in_half), grad_partial)
        blocks = z_blocks(
            [
                jnp.concatenate([partial[k * z_rows : (k + 1) * z_rows], sum_rows], 0)
                for k in range(z_size)
            ],
            (0, 1),
        )
        sums = [
            jnp.sum(block[z_rows : z_rows + 3, :units].astype(f32), 0, keepdims=True)
            for block in blocks
        ]
        blocks = [block[:z_rows] for block in blocks]
        pre_early, mean_early, scale_early = finish_pre(blocks, sums)
        grad_hidden_later = sum(block[:, :units].astype(f32) for block in blocks)
        hidden = gelu_value(pre_early).astype(bf16)
        hidden_early = z_gather(
            jnp.concatenate([hidden, pack_side([mean_early, scale_early])], 1), (0,)
        )
        branch = t_scatter(matmul(hidden_early[:, :units], w_out_pair).astype(bf16))
        middle_slab = (in_slab.astype(f32) + branch).astype(bf16)
        middle_slab = pick(middle_slab, section_hop(middle_slab, 0))
        middle = t_gather(middle_slab).reshape(half, pair_width)

    with jax.named_scope("tick1"):
        blocks = z_scatter(forward_partial(middle), (1,))
        pre_later, mean_later, scale_later = finish_pre(blocks, sums)
        hidden_share = gelu_value(pre_later).astype(bf16)
        grad_pre = (grad_hidden_later * gelu_slope(pre_later)).astype(bf16)
        side = pack_side([mean_later, scale_later, *backward_sums(grad_pre, pre_later)])
        grad_pre_later = z_gather(jnp.concatenate([grad_pre, side], 1), (1,))
        partial = matmul_t(grad_pre_later[:, :units], w_in_pair).astype(bf16)
        total = t_scatter(jnp.concatenate([partial, grad_pre_later[:, units:]], 1))
        turn_slab = input_gradient(in_slab, total, middle_slab, grad_pre_later[:, units:])
        turn_slab = pick(section_hop(turn_slab, 1), turn_slab)
        turn = t_gather(turn_slab).reshape(half, pair_width)

    with jax.named_scope("tick2"):
        blocks = z_scatter(matmul_t(turn, w_out_pair).astype(bf16), (0,))
        grad_hidden = sum(block.astype(f32) for block in blocks)
        grad_pre = (grad_hidden * gelu_slope(pre_early)).astype(bf16)
        side = pack_side([mean_early, scale_early, *backward_sums(grad_pre, pre_early)])
        share = jnp.concatenate([pick(grad_pre, hidden_share), side], 1)
        last = z_gather(share, (0, 1))
        partial = pick(
            matmul_t(last[:, :units], w_in_pair), matmul(last[:, :units], w_out_pair)
        ).astype(bf16)
        total = t_scatter(jnp.concatenate([partial, last[:, units:]], 1))
        final_slab = pick(
            input_gradient(turn_slab, total, in_slab, last[:, units:]),
            (middle_slab.astype(f32) + total[:, :pair_width]).astype(bf16),
        )
        final = t_gather(own_columns(final_slab).reshape(2, t_rows, own_width))
        final = jnp.swapaxes(final, 0, 1).reshape(rows, own_width)

    with jax.named_scope("weights"):
        middle_own = own_columns(middle)
        turn_own = own_columns(turn)
        grad_pre_half = pick(last, grad_pre_later)
        hidden_half = pick(hidden_early, last)
        grad_pre_all = jnp.concatenate([grad_pre_half, core_swap(grad_pre_half)], 0)
        hidden_all = jnp.concatenate([hidden_half, core_swap(hidden_half)], 0)
        side = grad_pre_all[:, units:]
        section_input = pick(in_own, middle_own).astype(f32)
        normed = ((section_input - side_value(side, 0)) * side_value(side, 1)).astype(bf16)
        grad_out = pick(turn_own, in_own)
        grad_w_in = matmul_ta(normed, grad_pre_all[:, :units]).astype(bf16)
        grad_w_out = matmul_ta(hidden_all[:, :units], grad_out).astype(bf16)

    shape = (1,) + tokens.shape
    return (
        reorder(pick(middle_own, final)).reshape(shape),
        reorder(pick(final, turn_own)).reshape(shape),
        grad_w_in[None],
        grad_w_out[None],
    )


def solution(mesh):
    in_specs = (
        P(None, None, "dp"),
        P("section", "dp", "tensor"),
        P("section", "tensor", "dp"),
        P(None, None, "dp"),
    )
    out_specs = (
        P("section", None, None, "dp"),
        P("section", None, None, "dp"),
        P("section", "dp", "tensor"),
        P("section", "tensor", "dp"),
    )
    return jax.shard_map(body, mesh=mesh, in_specs=in_specs, out_specs=out_specs, check_vma=False)
```

```python
import jax
import jax.numpy as jnp
from jax import lax
from jax.sharding import PartitionSpec as P

root_two_pi = 0.7978845608
LANES = 128
EVERYWHERE = ("section", "dp", "tensor")
STREAMS = 1
f32 = jnp.float32
bf16 = jnp.bfloat16


def gelu_value(pre_act):
    inner = jnp.tanh(root_two_pi * (pre_act + 0.044715 * pre_act**3))
    return 0.5 * pre_act * (1.0 + inner)


def gelu_slope(pre_act):
    inner = jnp.tanh(root_two_pi * (pre_act + 0.044715 * pre_act**3))
    return 0.5 * (1.0 + inner) + 0.5 * pre_act * (1.0 - inner * inner) * root_two_pi * (
        1.0 + 3.0 * 0.044715 * pre_act * pre_act
    )


def matmul(a, b):
    return jnp.dot(a, b, preferred_element_type=f32)


def matmul_t(a, b):
    return lax.dot_general(a, b, (((1,), (1,)), ((), ())), preferred_element_type=f32)


def matmul_ta(a, b):
    return lax.dot_general(a, b, (((0,), (0,)), ((), ())), preferred_element_type=f32)


def three_parts(value):
    high = lax.reduce_precision(value, 8, 7)
    rest = value - high
    middle = lax.reduce_precision(rest, 8, 7)
    return high, middle, rest - middle


def pack_side(columns):
    lane = lax.broadcasted_iota(jnp.int32, (1, LANES), 1)
    block = jnp.zeros((columns[0].shape[0], LANES), f32)
    for number, column in enumerate(columns):
        for part_no, part in enumerate(three_parts(column)):
            block = jnp.where(lane == 3 * number + part_no, part, block)
    return block.astype(bf16)


def side_value(block, number):
    lane = lax.broadcasted_iota(jnp.int32, block.shape, block.ndim - 1)
    kept = jnp.where(lane // 3 == number, block.astype(f32), 0.0)
    return jnp.sum(kept, axis=-1, keepdims=True)


def z_route(dp_size, tensor_size, sections, step):
    route = []
    for section in (0, 1):
        for place in range(dp_size):
            other = place ^ (2 * step) if section in sections else place ^ 1
            for column in range(tensor_size):
                route.append(
                    (
                        (section * dp_size + place) * tensor_size + column,
                        (section * dp_size + other) * tensor_size + column,
                    )
                )
    return route


def body(tokens, w_in, w_out, cotangent):
    dp_size = lax.axis_size("dp")
    tensor_size = lax.axis_size("tensor")
    z_size = dp_size // 2
    micro, rows_each, own_width = tokens.shape
    rows = micro * rows_each // STREAMS
    half = rows // 2
    z_rows = half // z_size
    t_rows = half // tensor_size
    width = own_width * dp_size
    pair_width = 2 * own_width
    units = w_in.shape[2]
    streams = range(STREAMS)
    first_section = lax.axis_index("section") == 0
    place = lax.axis_index("dp")
    z_place, core = place // 2, place % 2
    t_place = lax.axis_index("tensor")

    def pick(early, later):
        return jnp.where(first_section, early, later)

    def core_swap(block):
        return lax.ppermute(block, "dp", [(i, i ^ 1) for i in range(dp_size)])

    def section_hop(block, source):
        return lax.ppermute(block, "section", [(source, 1 - source)])

    def turn_axis(parts, axis, bit):
        low = lax.index_in_dim(parts, 0, axis)
        high = lax.index_in_dim(parts, 1, axis)
        return jnp.concatenate(
            [jnp.where(bit == 1, high, low), jnp.where(bit == 1, low, high)], axis
        )

    def turn_z(parts):
        return turn_axis(turn_axis(parts, 0, z_place // 2), 1, z_place % 2)

    def arrange(block):
        parts = turn_z(block.reshape(2, 2, tensor_size // 4, 2, t_rows, block.shape[1]))
        parts = turn_axis(parts, 3, core)
        return jnp.concatenate([parts[:, :, :, 0], parts[:, :, :, 1]], 0).reshape(block.shape)

    def arrange_back(block):
        parts = block.reshape(2, 2, 2, tensor_size // 4, t_rows, block.shape[1])
        parts = turn_axis(parts, 0, core)
        return turn_z(jnp.stack([parts[0], parts[1]], 3)).reshape(block.shape)

    def z_blocks(blocks, sections):
        return [blocks[0]] + [
            lax.ppermute(
                blocks[step], EVERYWHERE, z_route(dp_size, tensor_size, sections, step)
            )
            for step in range(1, z_size)
        ]

    def z_scatter(block, sections):
        return z_blocks([block[k * z_rows : (k + 1) * z_rows] for k in range(z_size)], sections)

    def z_gather(block, sections):
        return jnp.concatenate(z_blocks([block] * z_size, sections), 0)

    def t_scatter(block):
        blocks = block.reshape(tensor_size, t_rows, block.shape[1])
        parts = lax.all_to_all(blocks, "tensor", 0, 0)
        return jnp.sum(parts.astype(f32), 0)

    def t_gather(block):
        copies = jnp.broadcast_to(block[None], (tensor_size,) + block.shape)
        return lax.all_to_all(copies, "tensor", 0, 0)

    def t_slab(block):
        return lax.dynamic_slice_in_dim(block, t_place * t_rows, t_rows, 0)

    def own_columns(block):
        return jnp.concatenate([block[:, :own_width], core_swap(block[:, own_width:])], 0)

    def forward_partial(block):
        values = block.astype(f32)
        total = jnp.sum(values, 1, keepdims=True)
        squares = jnp.sum(values * values, 1, keepdims=True)
        product = matmul(block, w_in_pair) - (total / pair_width) * column_sum
        return jnp.concatenate([product.astype(bf16), pack_side([total, squares])], 1)

    def finish_pre(blocks, sums):
        sides = [block[:, units:] for block in blocks]
        totals = [side_value(side, 0) for side in sides]
        squares = sum(side_value(side, 1) for side in sides)
        mean = sum(totals) / width
        inv_scale = lax.rsqrt(squares / width - mean * mean + 1e-05)
        product = sum(block[:, :units].astype(f32) for block in blocks)
        for total, its_sum in zip(totals, sums):
            product = product + (total / pair_width - mean) * its_sum
        return product * inv_scale, mean, inv_scale

    def backward_sums(grad_pre, pre):
        values = grad_pre.astype(f32)
        first = jnp.sum(values * sum(sums), 1, keepdims=True)
        second = jnp.sum(values * pre, 1, keepdims=True)
        return first, second

    def input_gradient(grad_slab, total, input_slab, side):
        first = side_value(total[:, pair_width:], 2) / width
        second = side_value(total[:, pair_width:], 3) / width
        mean, inv_scale = side_value(t_slab(side), 0), side_value(t_slab(side), 1)
        normed = (input_slab.astype(f32) - mean) * inv_scale
        return (
            grad_slab.astype(f32) + inv_scale * (total[:, :pair_width] - first - normed * second)
        ).astype(bf16)

    with jax.named_scope("tick0"):
        w_in_own, w_out_own = w_in[0], w_out[0]
        w_in_pair = jnp.concatenate([w_in_own, core_swap(w_in_own)], 0)
        w_out_pair = jnp.concatenate([w_out_own, core_swap(w_out_own)], 1)
        column_sum = jnp.sum(w_in_pair.astype(f32), 0, keepdims=True)
        sum_rows = jnp.concatenate(
            list(three_parts(column_sum)) + [jnp.zeros((13, units), f32)], 0
        ).astype(bf16)
        sum_rows = jnp.concatenate([sum_rows, jnp.zeros((16, LANES), bf16)], 1)
        arriving = pick(tokens, cotangent).reshape(STREAMS, rows, own_width)
        in_own = [arrange(arriving[i]) for i in streams]
        in_half = [jnp.concatenate([own[:half], core_swap(own[half:])], 1) for own in in_own]
        in_slab = [t_slab(block) for block in in_half]
        early = []
        for i in streams:
            grad_partial = matmul_t(in_half[i], w_out_pair).astype(bf16)
            grad_partial = jnp.concatenate([grad_partial, jnp.zeros((half, LANES), bf16)], 1)
            partial = pick(forward_partial(in_half[i]), grad_partial)
            pieces = [partial[k * z_rows : (k + 1) * z_rows] for k in range(z_size)]
            if i == 0:
                pieces = [jnp.concatenate([piece, sum_rows], 0) for piece in pieces]
            early.append(z_blocks(pieces, (0, 1)))
        sums = [
            jnp.sum(block[z_rows : z_rows + 3, :units].astype(f32), 0, keepdims=True)
            for block in early[0]
        ]
        early[0] = [block[:z_rows] for block in early[0]]
        early_norm = [finish_pre(blocks, sums) for blocks in early]
        grad_hidden_later = [
            sum(block[:, :units].astype(f32) for block in blocks) for blocks in early
        ]
        hidden_early = [
            z_gather(
                jnp.concatenate(
                    [gelu_value(pre).astype(bf16), pack_side([mean, inv_scale])], 1
                ),
                (0,),
            )
            for pre, mean, inv_scale in early_norm
        ]
        middle_slab, middle = [], []
        for i in streams:
            branch = t_scatter(matmul(hidden_early[i][:, :units], w_out_pair).astype(bf16))
            slab = (in_slab[i].astype(f32) + branch).astype(bf16)
            slab = pick(slab, section_hop(slab, 0))
            middle_slab.append(slab)
            middle.append(t_gather(slab).reshape(half, pair_width))

    with jax.named_scope("tick1"):
        hidden_share, grad_pre_later, turn_slab, turn = [], [], [], []
        for i in streams:
            blocks = z_scatter(forward_partial(middle[i]), (1,))
            pre, mean, inv_scale = finish_pre(blocks, sums)
            hidden_share.append(gelu_value(pre).astype(bf16))
            grad_pre = (grad_hidden_later[i] * gelu_slope(pre)).astype(bf16)
            side = pack_side([mean, inv_scale, *backward_sums(grad_pre, pre)])
            grad_pre_later.append(z_gather(jnp.concatenate([grad_pre, side], 1), (1,)))
        for i in streams:
            side = grad_pre_later[i][:, units:]
            partial = matmul_t(grad_pre_later[i][:, :units], w_in_pair).astype(bf16)
            total = t_scatter(jnp.concatenate([partial, side], 1))
            slab = input_gradient(in_slab[i], total, middle_slab[i], side)
            slab = pick(section_hop(slab, 1), slab)
            turn_slab.append(slab)
            turn.append(t_gather(slab).reshape(half, pair_width))

    with jax.named_scope("tick2"):
        last, totals = [], []
        for i in streams:
            blocks = z_scatter(matmul_t(turn[i], w_out_pair).astype(bf16), (0,))
            grad_hidden = sum(block.astype(f32) for block in blocks)
            pre, mean, inv_scale = early_norm[i]
            grad_pre = (grad_hidden * gelu_slope(pre)).astype(bf16)
            side = pack_side([mean, inv_scale, *backward_sums(grad_pre, pre)])
            share = jnp.concatenate([pick(grad_pre, hidden_share[i]), side], 1)
            last.append(z_gather(share, (0, 1)))
        for i in streams:
            partial = pick(
                matmul_t(last[i][:, :units], w_in_pair), matmul(last[i][:, :units], w_out_pair)
            ).astype(bf16)
            totals.append(t_scatter(jnp.concatenate([partial, last[i][:, units:]], 1)))

    with jax.named_scope("weights"):
        middle_own = [own_columns(block) for block in middle]
        turn_own = [own_columns(block) for block in turn]

        def both_halves(early_halves, later_halves):
            halves = [pick(*pair) for pair in zip(early_halves, later_halves)]
            return jnp.concatenate([x for h in halves for x in (h, core_swap(h))], 0)

        grad_pre_all = both_halves(last, grad_pre_later)
        hidden_all = both_halves(hidden_early, last)
        side = grad_pre_all[:, units:]
        own_input = jnp.concatenate(in_own, 0)
        section_input = pick(own_input, jnp.concatenate(middle_own, 0)).astype(f32)
        normed = ((section_input - side_value(side, 0)) * side_value(side, 1)).astype(bf16)
        grad_out = pick(jnp.concatenate(turn_own, 0), own_input)
        grad_w_out = matmul_ta(hidden_all[:, :units], grad_out).astype(bf16)
        grad_w_in = matmul_ta(normed, grad_pre_all[:, :units]).astype(bf16)

    with jax.named_scope("last"):
        totals[-1], grad_w_out, normed = lax.optimization_barrier((totals[-1], grad_w_out, normed))
        final = []
        for i in streams:
            slab = pick(
                input_gradient(turn_slab[i], totals[i], in_slab[i], last[i][:, units:]),
                (middle_slab[i].astype(f32) + totals[i][:, :pair_width]).astype(bf16),
            )
            pair = turn_axis(own_columns(slab).reshape(2, t_rows, own_width), 0, core)
            final.append(t_gather(pair))
        final[-1], grad_w_in = lax.optimization_barrier((final[-1], grad_w_in))
        final = [
            turn_z(x.reshape(2, 2, tensor_size // 4, 2, t_rows, own_width)).reshape(rows, own_width)
            for x in final
        ]

    shape = (1,) + tokens.shape
    middle_out = jnp.concatenate([arrange_back(block) for block in middle_own], 0)
    turn_out = jnp.concatenate([arrange_back(block) for block in turn_own], 0)
    final_out = jnp.concatenate(final, 0)
    return (
        pick(middle_out, final_out).reshape(shape),
        pick(final_out, turn_out).reshape(shape),
        grad_w_in[None],
        grad_w_out[None],
    )


def solution(mesh):
    in_specs = (
        P(None, None, "dp"),
        P("section", "dp", "tensor"),
        P("section", "tensor", "dp"),
        P(None, None, "dp"),
    )
    out_specs = (
        P("section", None, None, "dp"),
        P("section", None, None, "dp"),
        P("section", "dp", "tensor"),
        P("section", "tensor", "dp"),
    )
    return jax.shard_map(body, mesh=mesh, in_specs=in_specs, out_specs=out_specs, check_vma=False)
```

```python
import jax
import jax.numpy as jnp
import numpy as np
from jax import lax
from jax.sharding import PartitionSpec as P

root_two_pi = 0.7978845608
LANES = 128
EVERYWHERE = ("section", "dp", "tensor")
STREAMS = 1
f32 = jnp.float32
bf16 = jnp.bfloat16


def gelu_value(pre_act):
    inner = jnp.tanh(root_two_pi * (pre_act + 0.044715 * pre_act**3))
    return 0.5 * pre_act * (1.0 + inner)


def gelu_slope(pre_act):
    inner = jnp.tanh(root_two_pi * (pre_act + 0.044715 * pre_act**3))
    return 0.5 * (1.0 + inner) + 0.5 * pre_act * (1.0 - inner * inner) * root_two_pi * (
        1.0 + 3.0 * 0.044715 * pre_act * pre_act
    )


def matmul(a, b):
    return jnp.dot(a, b, preferred_element_type=f32)


def matmul_t(a, b):
    return lax.dot_general(a, b, (((1,), (1,)), ((), ())), preferred_element_type=f32)


def matmul_ta(a, b):
    return lax.dot_general(a, b, (((0,), (0,)), ((), ())), preferred_element_type=f32)


def three_parts(value):
    high = lax.reduce_precision(value, 8, 7)
    rest = value - high
    middle = lax.reduce_precision(rest, 8, 7)
    return high, middle, rest - middle


def lane_mask(first, count):
    mask = np.zeros((1, LANES), np.float32)
    mask[0, first : first + count] = 1.0
    return mask


def pack_side(columns):
    block = 0.0
    for number, column in enumerate(columns):
        for part_no, part in enumerate(three_parts(column)):
            block = block + part * lane_mask(3 * number + part_no, 1)
    return block.astype(bf16)


def side_value(block, number):
    return jnp.sum(block.astype(f32) * lane_mask(3 * number, 3), axis=-1, keepdims=True)


def z_route(dp_size, tensor_size, sections, step):
    route = []
    for section in (0, 1):
        for place in range(dp_size):
            other = place ^ (2 * step) if section in sections else place ^ 1
            for column in range(tensor_size):
                route.append(
                    (
                        (section * dp_size + place) * tensor_size + column,
                        (section * dp_size + other) * tensor_size + column,
                    )
                )
    return route


def body(tokens, w_in, w_out, cotangent):
    dp_size = lax.axis_size("dp")
    tensor_size = lax.axis_size("tensor")
    z_size = dp_size // 2
    micro, rows_each, own_width = tokens.shape
    rows = micro * rows_each // STREAMS
    half = rows // 2
    z_rows = half // z_size
    t_rows = half // tensor_size
    width = own_width * dp_size
    pair_width = 2 * own_width
    units = w_in.shape[2]
    streams = range(STREAMS)
    first_section = lax.axis_index("section") == 0
    place = lax.axis_index("dp")
    z_place, core = place // 2, place % 2
    t_place = lax.axis_index("tensor")

    def pick(early, later):
        return jnp.where(first_section, early, later)

    def core_swap(block):
        return lax.ppermute(block, "dp", [(i, i ^ 1) for i in range(dp_size)])

    def section_hop(block, source):
        return lax.ppermute(block, "section", [(source, 1 - source)])

    def turn_axis(parts, axis, bit):
        low = lax.index_in_dim(parts, 0, axis)
        high = lax.index_in_dim(parts, 1, axis)
        return jnp.concatenate(
            [jnp.where(bit == 1, high, low), jnp.where(bit == 1, low, high)], axis
        )

    def turn_z(parts):
        return turn_axis(turn_axis(parts, 0, z_place // 2), 1, z_place % 2)

    def arrange(block):
        parts = turn_z(block.reshape(2, 2, tensor_size // 4, 2, t_rows, block.shape[1]))
        parts = turn_axis(parts, 3, core)
        return jnp.concatenate([parts[:, :, :, 0], parts[:, :, :, 1]], 0).reshape(block.shape)

    def arrange_back(block):
        parts = block.reshape(2, 2, 2, tensor_size // 4, t_rows, block.shape[1])
        parts = turn_axis(parts, 0, core)
        return turn_z(jnp.stack([parts[0], parts[1]], 3)).reshape(block.shape)

    def z_blocks(blocks, sections):
        return [blocks[0]] + [
            lax.ppermute(
                blocks[step], EVERYWHERE, z_route(dp_size, tensor_size, sections, step)
            )
            for step in range(1, z_size)
        ]

    def z_scatter(block, sections):
        return z_blocks([block[k * z_rows : (k + 1) * z_rows] for k in range(z_size)], sections)

    def z_gather(block, sections):
        return jnp.concatenate(z_blocks([block] * z_size, sections), 0)

    def t_scatter(block, *ready):
        block, *ready = lax.optimization_barrier((block, *ready))
        blocks = block.reshape(tensor_size, t_rows, block.shape[1])
        parts = lax.all_to_all(blocks, "tensor", 0, 0)
        return jnp.sum(parts.astype(f32), 0), *ready

    def t_gather(block):
        copies = jnp.broadcast_to(block[None], (tensor_size,) + block.shape)
        return lax.all_to_all(copies, "tensor", 0, 0)

    def t_slab(block):
        return lax.dynamic_slice_in_dim(block, t_place * t_rows, t_rows, 0)

    def own_columns(block):
        return jnp.concatenate([block[:, :own_width], core_swap(block[:, own_width:])], 0)

    def forward_partial(block):
        values = block.astype(f32)
        total = jnp.sum(values, 1, keepdims=True)
        squares = jnp.sum(values * values, 1, keepdims=True)
        product = matmul(block, w_in_pair) - (total / pair_width) * column_sum
        return jnp.concatenate([product.astype(bf16), pack_side([total, squares])], 1)

    def finish_pre(blocks, sums):
        sides = [block[:, units:] for block in blocks]
        totals = [side_value(side, 0) for side in sides]
        squares = sum(side_value(side, 1) for side in sides)
        mean = sum(totals) / width
        inv_scale = lax.rsqrt(squares / width - mean * mean + 1e-05)
        product = sum(block[:, :units].astype(f32) for block in blocks)
        for total, its_sum in zip(totals, sums):
            product = product + (total / pair_width - mean) * its_sum
        return product * inv_scale, mean, inv_scale

    def backward_sums(grad_pre, pre):
        values = grad_pre.astype(f32)
        first = jnp.sum(values * sum(sums), 1, keepdims=True)
        second = jnp.sum(values * pre, 1, keepdims=True)
        return first, second

    def slab_norm(side):
        return side_value(t_slab(side), 0), side_value(t_slab(side), 1)

    def input_gradient(grad_slab, total, input_slab, mean, inv_scale):
        first = side_value(total[:, pair_width:], 2) / width
        second = side_value(total[:, pair_width:], 3) / width
        normed = (input_slab.astype(f32) - mean) * inv_scale
        return (
            grad_slab.astype(f32) + inv_scale * (total[:, :pair_width] - first - normed * second)
        ).astype(bf16)

    with jax.named_scope("tick0"):
        w_in_own, w_out_own = w_in[0], w_out[0]
        w_in_pair = jnp.concatenate([w_in_own, core_swap(w_in_own)], 0)
        w_out_pair = jnp.concatenate([w_out_own, core_swap(w_out_own)], 1)
        column_sum = matmul(jnp.ones((16, pair_width), bf16), w_in_pair)[:1]
        sum_rows = jnp.concatenate(
            list(three_parts(column_sum)) + [jnp.zeros((13, units), f32)], 0
        ).astype(bf16)
        sum_rows = jnp.concatenate([sum_rows, jnp.zeros((16, LANES), bf16)], 1)
        arriving = pick(tokens, cotangent).reshape(STREAMS, rows, own_width)
        in_own = [arrange(arriving[i]) for i in streams]
        in_half = [jnp.concatenate([own[:half], core_swap(own[half:])], 1) for own in in_own]
        in_slab = [t_slab(block) for block in in_half]
        early = []
        for i in streams:
            partial = forward_partial(in_half[i])
            pieces = [partial[k * z_rows : (k + 1) * z_rows] for k in range(z_size)]
            if i == 0:
                pieces = [jnp.concatenate([piece, sum_rows], 0) for piece in pieces]
            early.append(z_blocks(pieces, (0,)))
        sums = [
            jnp.sum(block[z_rows : z_rows + 3, :units].astype(f32), 0, keepdims=True)
            for block in early[0]
        ]
        early[0] = [block[:z_rows] for block in early[0]]
        early_norm = [finish_pre(blocks, sums) for blocks in early]
        sum_tiles = units // LANES
        sum_block = jnp.concatenate(
            [part.reshape(sum_tiles, LANES) for part in three_parts(column_sum)]
            + [jnp.zeros((z_rows - 3 * sum_tiles, LANES), f32)],
            0,
        ).astype(bf16)
        hidden_early, grad_hidden_later = [], []
        for i in streams:
            pre, mean, inv_scale = early_norm[i]
            share = jnp.concatenate(
                [gelu_value(pre).astype(bf16), pack_side([mean, inv_scale])], 1
            )
            grads = matmul_t(in_half[i], w_out_pair).astype(bf16)
            grads = [
                jnp.concatenate([grads[k * z_rows : (k + 1) * z_rows], sum_block], 1)
                for k in range(z_size)
            ]
            blocks = z_blocks([pick(share, block) for block in grads], (0, 1))
            if i == 0:
                sent = [block[: 3 * sum_tiles, units:].astype(f32) for block in blocks]
                sent = [jnp.sum(x.reshape(3, sum_tiles, LANES), 0) for x in sent]
                sums = [pick(a, x.reshape(1, units)) for a, x in zip(sums, sent)]
            hidden_early.append(jnp.concatenate(blocks, 0))
            grad_hidden_later.append(sum(block[:, :units].astype(f32) for block in blocks))
        middle_slab, middle = [], []
        for i in streams:
            branch, in_slab[i] = t_scatter(
                matmul(hidden_early[i][:, :units], w_out_pair).astype(bf16), in_slab[i]
            )
            slab = (in_slab[i].astype(f32) + branch).astype(bf16)
            slab = pick(slab, section_hop(slab, 0))
            middle_slab.append(slab)
            middle.append(t_gather(slab).reshape(half, pair_width))

    with jax.named_scope("tick1"):
        hidden_share, grad_pre_later, turn_slab, turn = [], [], [], []
        for i in streams:
            blocks = z_scatter(forward_partial(middle[i]), (1,))
            pre, mean, inv_scale = finish_pre(blocks, sums)
            hidden_share.append(gelu_value(pre).astype(bf16))
            grad_pre = (grad_hidden_later[i] * gelu_slope(pre)).astype(bf16)
            side = pack_side([mean, inv_scale, *backward_sums(grad_pre, pre)])
            grad_pre_later.append(z_gather(jnp.concatenate([grad_pre, side], 1), (1,)))
        for i in streams:
            side = grad_pre_later[i][:, units:]
            partial = matmul_t(grad_pre_later[i][:, :units], w_in_pair).astype(bf16)
            total, *norm = t_scatter(jnp.concatenate([partial, side], 1), *slab_norm(side))
            slab = input_gradient(in_slab[i], total, middle_slab[i], *norm)
            slab = pick(section_hop(slab, 1), slab)
            turn_slab.append(slab)
            turn.append(t_gather(slab).reshape(half, pair_width))

    with jax.named_scope("tick2"):
        last, totals, last_norm = [], [], []
        for i in streams:
            blocks = z_scatter(matmul_t(turn[i], w_out_pair).astype(bf16), (0,))
            grad_hidden = sum(block.astype(f32) for block in blocks)
            pre, mean, inv_scale = early_norm[i]
            grad_pre = (grad_hidden * gelu_slope(pre)).astype(bf16)
            side = pack_side([mean, inv_scale, *backward_sums(grad_pre, pre)])
            share = jnp.concatenate([pick(grad_pre, hidden_share[i]), side], 1)
            last.append(z_gather(share, (0, 1)))
        for i in streams:
            partial = pick(
                matmul_t(last[i][:, :units], w_in_pair), matmul(last[i][:, :units], w_out_pair)
            ).astype(bf16)
            side = last[i][:, units:]
            total, *norm = t_scatter(jnp.concatenate([partial, side], 1), *slab_norm(side))
            totals.append(total)
            last_norm.append(norm)

    with jax.named_scope("weights"):
        middle_own = [own_columns(block) for block in middle]
        turn_own = [own_columns(block) for block in turn]

        def both_halves(early_halves, later_halves):
            halves = [pick(*pair) for pair in zip(early_halves, later_halves)]
            return jnp.concatenate([x for h in halves for x in (h, core_swap(h))], 0)

        grad_pre_all = both_halves(last, grad_pre_later)
        hidden_all = both_halves(hidden_early, last)
        side = grad_pre_all[:, units:]
        own_input = jnp.concatenate(in_own, 0)
        section_input = pick(own_input, jnp.concatenate(middle_own, 0)).astype(f32)
        normed = ((section_input - side_value(side, 0)) * side_value(side, 1)).astype(bf16)
        grad_out = pick(jnp.concatenate(turn_own, 0), own_input)
        grad_w_out = matmul_ta(hidden_all[:, :units], grad_out).astype(bf16)
        grad_w_in = matmul_ta(normed, grad_pre_all[:, :units]).astype(bf16)

    with jax.named_scope("last"):
        totals[-1], grad_w_out, normed = lax.optimization_barrier((totals[-1], grad_w_out, normed))
        final = []
        for i in streams:
            slab = pick(
                input_gradient(turn_slab[i], totals[i], in_slab[i], *last_norm[i]),
                (middle_slab[i].astype(f32) + totals[i][:, :pair_width]).astype(bf16),
            )
            pair = turn_axis(own_columns(slab).reshape(2, t_rows, own_width), 0, core)
            final.append(t_gather(pair))
        final[-1], grad_w_in = lax.optimization_barrier((final[-1], grad_w_in))
        final = [
            turn_z(x.reshape(2, 2, tensor_size // 4, 2, t_rows, own_width)).reshape(rows, own_width)
            for x in final
        ]

    shape = (1,) + tokens.shape
    middle_out = jnp.concatenate([arrange_back(block) for block in middle_own], 0)
    turn_out = jnp.concatenate([arrange_back(block) for block in turn_own], 0)
    final_out = jnp.concatenate(final, 0)
    return (
        pick(middle_out, final_out).reshape(shape),
        pick(final_out, turn_out).reshape(shape),
        grad_w_in[None],
        grad_w_out[None],
    )


def solution(mesh):
    in_specs = (
        P(None, None, "dp"),
        P("section", "dp", "tensor"),
        P("section", "tensor", "dp"),
        P(None, None, "dp"),
    )
    out_specs = (
        P("section", None, None, "dp"),
        P("section", None, None, "dp"),
        P("section", "dp", "tensor"),
        P("section", "tensor", "dp"),
    )
    return jax.shard_map(body, mesh=mesh, in_specs=in_specs, out_specs=out_specs, check_vma=False)
```

```python
import jax
import jax.numpy as jnp
import numpy as np
from jax import lax
from jax.sharding import PartitionSpec as P

root_two_pi = 0.7978845608
LANES = 128
EVERYWHERE = ("section", "dp", "tensor")
STREAMS = 1
f32 = jnp.float32
bf16 = jnp.bfloat16


def gelu_value(pre_act):
    inner = jnp.tanh(root_two_pi * (pre_act + 0.044715 * pre_act**3))
    return 0.5 * pre_act * (1.0 + inner)


def gelu_slope(pre_act):
    inner = jnp.tanh(root_two_pi * (pre_act + 0.044715 * pre_act**3))
    return 0.5 * (1.0 + inner) + 0.5 * pre_act * (1.0 - inner * inner) * root_two_pi * (
        1.0 + 3.0 * 0.044715 * pre_act * pre_act
    )


def matmul(a, b):
    return jnp.dot(a, b, preferred_element_type=f32)


def matmul_t(a, b):
    return lax.dot_general(a, b, (((1,), (1,)), ((), ())), preferred_element_type=f32)


def matmul_ta(a, b):
    return lax.dot_general(a, b, (((0,), (0,)), ((), ())), preferred_element_type=f32)


def three_parts(value):
    high = lax.reduce_precision(value, 8, 7)
    rest = value - high
    middle = lax.reduce_precision(rest, 8, 7)
    return high, middle, rest - middle


def lane_mask(first, count):
    mask = np.zeros((1, LANES), np.float32)
    mask[0, first : first + count] = 1.0
    return mask


def pack_side(columns):
    block = 0.0
    for number, column in enumerate(columns):
        for part_no, part in enumerate(three_parts(column)):
            block = block + part * lane_mask(3 * number + part_no, 1)
    return block.astype(bf16)


def side_value(block, number):
    return jnp.sum(block.astype(f32) * lane_mask(3 * number, 3), axis=-1, keepdims=True)


def z_route(dp_size, tensor_size, sections, step):
    route = []
    for section in (0, 1):
        for place in range(dp_size):
            other = place ^ (2 * step) if section in sections else place ^ 1
            for column in range(tensor_size):
                route.append(
                    (
                        (section * dp_size + place) * tensor_size + column,
                        (section * dp_size + other) * tensor_size + column,
                    )
                )
    return route


def body(tokens, w_in, w_out, cotangent):
    dp_size = lax.axis_size("dp")
    tensor_size = lax.axis_size("tensor")
    z_size = dp_size // 2
    micro, rows_each, own_width = tokens.shape
    rows = micro * rows_each // STREAMS
    half = rows // 2
    z_rows = half // z_size
    t_rows = half // tensor_size
    width = own_width * dp_size
    pair_width = 2 * own_width
    units = w_in.shape[2]
    streams = range(STREAMS)
    first_section = lax.axis_index("section") == 0
    place = lax.axis_index("dp")
    z_place, core = place // 2, place % 2
    t_place = lax.axis_index("tensor")

    def pick(early, later):
        return jnp.where(first_section, early, later)

    def core_swap(block):
        return lax.ppermute(block, "dp", [(i, i ^ 1) for i in range(dp_size)])

    def section_hop(block, source):
        return lax.ppermute(block, "section", [(source, 1 - source)])

    def turn_axis(parts, axis, bit):
        low = lax.index_in_dim(parts, 0, axis)
        high = lax.index_in_dim(parts, 1, axis)
        return jnp.concatenate(
            [jnp.where(bit == 1, high, low), jnp.where(bit == 1, low, high)], axis
        )

    def turn_z(parts):
        return turn_axis(turn_axis(parts, 0, z_place // 2), 1, z_place % 2)

    def arrange(block):
        parts = turn_z(block.reshape(2, 2, tensor_size // 4, 2, t_rows, block.shape[1]))
        parts = turn_axis(parts, 3, core)
        return jnp.concatenate([parts[:, :, :, 0], parts[:, :, :, 1]], 0).reshape(block.shape)

    def arrange_back(block):
        parts = block.reshape(2, 2, 2, tensor_size // 4, t_rows, block.shape[1])
        parts = turn_axis(parts, 0, core)
        return turn_z(jnp.stack([parts[0], parts[1]], 3)).reshape(block.shape)

    def z_blocks(blocks, sections):
        return [blocks[0]] + [
            lax.ppermute(
                blocks[step], EVERYWHERE, z_route(dp_size, tensor_size, sections, step)
            )
            for step in range(1, z_size)
        ]

    def z_scatter(block, sections):
        return z_blocks([block[k * z_rows : (k + 1) * z_rows] for k in range(z_size)], sections)

    def z_gather(block, sections):
        return jnp.concatenate(z_blocks([block] * z_size, sections), 0)

    def t_scatter(block, *ready):
        block, *ready = lax.optimization_barrier((block, *ready))
        blocks = block.reshape(tensor_size, t_rows, block.shape[1])
        parts = lax.all_to_all(blocks, "tensor", 0, 0)
        return jnp.sum(parts.astype(f32), 0), *ready

    def t_gather(block):
        copies = jnp.broadcast_to(block[None], (tensor_size,) + block.shape)
        return lax.all_to_all(copies, "tensor", 0, 0)

    def t_slab(block):
        return lax.dynamic_slice_in_dim(block, t_place * t_rows, t_rows, 0)

    def own_columns(block):
        return jnp.concatenate([block[:, :own_width], core_swap(block[:, own_width:])], 0)

    def forward_partial(block):
        values = block.astype(f32)
        total = jnp.sum(values, 1, keepdims=True)
        squares = jnp.sum(values * values, 1, keepdims=True)
        product = matmul(block, w_in_pair) - (total / pair_width) * column_sum
        return jnp.concatenate([product.astype(bf16), pack_side([total, squares])], 1)

    def finish_pre(blocks, sums):
        sides = [block[:, units:] for block in blocks]
        totals = [side_value(side, 0) for side in sides]
        squares = sum(side_value(side, 1) for side in sides)
        mean = sum(totals) / width
        inv_scale = lax.rsqrt(squares / width - mean * mean + 1e-05)
        product = sum(block[:, :units].astype(f32) for block in blocks)
        for total, its_sum in zip(totals, sums):
            product = product + (total / pair_width - mean) * its_sum
        return product * inv_scale, mean, inv_scale

    def backward_sums(grad_pre, pre):
        values = grad_pre.astype(f32)
        first = jnp.sum(values * sum(sums), 1, keepdims=True)
        second = jnp.sum(values * pre, 1, keepdims=True)
        return first, second

    def slab_norm(side):
        return side_value(t_slab(side), 0), side_value(t_slab(side), 1)

    def input_gradient(grad_slab, total, input_slab, mean, inv_scale):
        first = side_value(total[:, pair_width:], 2) / width
        second = side_value(total[:, pair_width:], 3) / width
        normed = (input_slab.astype(f32) - mean) * inv_scale
        return (
            grad_slab.astype(f32) + inv_scale * (total[:, :pair_width] - first - normed * second)
        ).astype(bf16)

    with jax.named_scope("tick0"):
        w_in_own, w_out_own = w_in[0], w_out[0]
        w_in_pair = jnp.concatenate([w_in_own, core_swap(w_in_own)], 0)
        w_out_pair = jnp.concatenate([w_out_own, core_swap(w_out_own)], 1)
        w_in_pair = lax.optimization_barrier(w_in_pair)
        w_out_pair = lax.optimization_barrier(w_out_pair)
        column_sum = matmul(jnp.ones((16, pair_width), bf16), w_in_pair)[:1]
        sum_rows = jnp.concatenate(
            list(three_parts(column_sum)) + [jnp.zeros((13, units), f32)], 0
        ).astype(bf16)
        sum_rows = jnp.concatenate([sum_rows, jnp.zeros((16, LANES), bf16)], 1)
        arriving = pick(tokens, cotangent).reshape(STREAMS, rows, own_width)
        in_own = [arrange(arriving[i]) for i in streams]
        in_half = [jnp.concatenate([own[:half], core_swap(own[half:])], 1) for own in in_own]
        in_slab = [t_slab(block) for block in in_half]
        early = []
        for i in streams:
            partial = forward_partial(in_half[i])
            pieces = [partial[k * z_rows : (k + 1) * z_rows] for k in range(z_size)]
            if i == 0:
                pieces = [jnp.concatenate([piece, sum_rows], 0) for piece in pieces]
            early.append(z_blocks(pieces, (0,)))
        sums = [
            jnp.sum(block[z_rows : z_rows + 3, :units].astype(f32), 0, keepdims=True)
            for block in early[0]
        ]
        early[0] = [block[:z_rows] for block in early[0]]
        early_norm = [finish_pre(blocks, sums) for blocks in early]
        sum_tiles = units // LANES
        sum_block = jnp.concatenate(
            [part.reshape(sum_tiles, LANES) for part in three_parts(column_sum)]
            + [jnp.zeros((z_rows - 3 * sum_tiles, LANES), f32)],
            0,
        ).astype(bf16)
        hidden_early, grad_hidden_later = [], []
        for i in streams:
            pre, mean, inv_scale = early_norm[i]
            share = jnp.concatenate(
                [gelu_value(pre).astype(bf16), pack_side([mean, inv_scale])], 1
            )
            grads = matmul_t(in_half[i], w_out_pair).astype(bf16)
            grads = [
                jnp.concatenate([grads[k * z_rows : (k + 1) * z_rows], sum_block], 1)
                for k in range(z_size)
            ]
            blocks = z_blocks([pick(share, block) for block in grads], (0, 1))
            if i == 0:
                sent = [block[: 3 * sum_tiles, units:].astype(f32) for block in blocks]
                sent = [jnp.sum(x.reshape(3, sum_tiles, LANES), 0) for x in sent]
                sums = [pick(a, x.reshape(1, units)) for a, x in zip(sums, sent)]
            hidden_early.append(jnp.concatenate(blocks, 0))
            grad_hidden_later.append(sum(block[:, :units].astype(f32) for block in blocks))
        middle_slab, middle = [], []
        for i in streams:
            branch, in_slab[i] = t_scatter(
                matmul(hidden_early[i][:, :units], w_out_pair).astype(bf16), in_slab[i]
            )
            slab = (in_slab[i].astype(f32) + branch).astype(bf16)
            slab = pick(slab, section_hop(slab, 0))
            middle_slab.append(slab)
            middle.append(t_gather(slab).reshape(half, pair_width))

    with jax.named_scope("tick1"):
        hidden_share, grad_pre_later, turn_slab, turn = [], [], [], []
        for i in streams:
            blocks = z_scatter(forward_partial(middle[i]), (1,))
            pre, mean, inv_scale = finish_pre(blocks, sums)
            hidden_share.append(gelu_value(pre).astype(bf16))
            grad_pre = (grad_hidden_later[i] * gelu_slope(pre)).astype(bf16)
            side = pack_side([mean, inv_scale, *backward_sums(grad_pre, pre)])
            grad_pre_later.append(z_gather(jnp.concatenate([grad_pre, side], 1), (1,)))
        for i in streams:
            side = grad_pre_later[i][:, units:]
            partial = matmul_t(grad_pre_later[i][:, :units], w_in_pair).astype(bf16)
            total, *norm = t_scatter(jnp.concatenate([partial, side], 1), *slab_norm(side))
            slab = input_gradient(in_slab[i], total, middle_slab[i], *norm)
            slab = pick(section_hop(slab, 1), slab)
            turn_slab.append(slab)
            turn.append(t_gather(slab).reshape(half, pair_width))

    with jax.named_scope("tick2"):
        last, totals, last_norm = [], [], []
        for i in streams:
            blocks = z_scatter(matmul_t(turn[i], w_out_pair).astype(bf16), (0,))
            grad_hidden = sum(block.astype(f32) for block in blocks)
            pre, mean, inv_scale = early_norm[i]
            grad_pre = (grad_hidden * gelu_slope(pre)).astype(bf16)
            side = pack_side([mean, inv_scale, *backward_sums(grad_pre, pre)])
            share = jnp.concatenate([pick(grad_pre, hidden_share[i]), side], 1)
            last.append(z_gather(share, (0, 1)))
        for i in streams:
            partial = pick(
                matmul_t(last[i][:, :units], w_in_pair), matmul(last[i][:, :units], w_out_pair)
            ).astype(bf16)
            side = last[i][:, units:]
            total, *norm = t_scatter(jnp.concatenate([partial, side], 1), *slab_norm(side))
            totals.append(total)
            last_norm.append(norm)

    with jax.named_scope("weights"):
        middle_own = [own_columns(block) for block in middle]
        turn_own = [own_columns(block) for block in turn]

        def both_halves(early_halves, later_halves):
            halves = [pick(*pair) for pair in zip(early_halves, later_halves)]
            return jnp.concatenate([x for h in halves for x in (h, core_swap(h))], 0)

        grad_pre_all = both_halves(last, grad_pre_later)
        hidden_all = both_halves(hidden_early, last)
        side = grad_pre_all[:, units:]
        own_input = jnp.concatenate(in_own, 0)
        section_input = pick(own_input, jnp.concatenate(middle_own, 0)).astype(f32)
        normed = ((section_input - side_value(side, 0)) * side_value(side, 1)).astype(bf16)
        grad_out = pick(jnp.concatenate(turn_own, 0), own_input)
        grad_w_out = matmul_ta(hidden_all[:, :units], grad_out).astype(bf16)
        grad_w_in = matmul_ta(normed, grad_pre_all[:, :units]).astype(bf16)

    with jax.named_scope("last"):
        totals[-1], grad_w_out, normed = lax.optimization_barrier((totals[-1], grad_w_out, normed))
        final = []
        for i in streams:
            slab = pick(
                input_gradient(turn_slab[i], totals[i], in_slab[i], *last_norm[i]),
                (middle_slab[i].astype(f32) + totals[i][:, :pair_width]).astype(bf16),
            )
            pair = turn_axis(own_columns(slab).reshape(2, t_rows, own_width), 0, core)
            final.append(t_gather(pair))
        final[-1], grad_w_in = lax.optimization_barrier((final[-1], grad_w_in))
        final = [
            turn_z(x.reshape(2, 2, tensor_size // 4, 2, t_rows, own_width)).reshape(rows, own_width)
            for x in final
        ]

    shape = (1,) + tokens.shape
    middle_out = jnp.concatenate([arrange_back(block) for block in middle_own], 0)
    turn_out = jnp.concatenate([arrange_back(block) for block in turn_own], 0)
    final_out = jnp.concatenate(final, 0)
    return (
        pick(middle_out, final_out).reshape(shape),
        pick(final_out, turn_out).reshape(shape),
        grad_w_in[None],
        grad_w_out[None],
    )


def solution(mesh):
    in_specs = (
        P(None, None, "dp"),
        P("section", "dp", "tensor"),
        P("section", "tensor", "dp"),
        P(None, None, "dp"),
    )
    out_specs = (
        P("section", None, None, "dp"),
        P("section", None, None, "dp"),
        P("section", "dp", "tensor"),
        P("section", "tensor", "dp"),
    )
    return jax.shard_map(body, mesh=mesh, in_specs=in_specs, out_specs=out_specs, check_vma=False)
```

```python
import jax
import jax.numpy as jnp
import numpy as np
from jax import lax
from jax.sharding import PartitionSpec as P

root_two_pi = 0.7978845608
LANES = 128
EVERYWHERE = ("section", "dp", "tensor")
STREAMS = 1
f32 = jnp.float32
bf16 = jnp.bfloat16


def gelu_value(pre_act):
    inner = jnp.tanh(root_two_pi * (pre_act + 0.044715 * pre_act**3))
    return 0.5 * pre_act * (1.0 + inner)


def gelu_slope(pre_act):
    inner = jnp.tanh(root_two_pi * (pre_act + 0.044715 * pre_act**3))
    return 0.5 * (1.0 + inner) + 0.5 * pre_act * (1.0 - inner * inner) * root_two_pi * (
        1.0 + 3.0 * 0.044715 * pre_act * pre_act
    )


def matmul(a, b):
    return jnp.dot(a, b, preferred_element_type=f32)


def matmul_t(a, b):
    return lax.dot_general(a, b, (((1,), (1,)), ((), ())), preferred_element_type=f32)


def matmul_ta(a, b):
    return lax.dot_general(a, b, (((0,), (0,)), ((), ())), preferred_element_type=f32)


def three_parts(value):
    high = lax.reduce_precision(value, 8, 7)
    rest = value - high
    middle = lax.reduce_precision(rest, 8, 7)
    return high, middle, rest - middle


def lane_mask(first, count):
    mask = np.zeros((1, LANES), np.float32)
    mask[0, first : first + count] = 1.0
    return mask


def pack_side(columns):
    block = 0.0
    for number, column in enumerate(columns):
        for part_no, part in enumerate(three_parts(column)):
            block = block + part * lane_mask(3 * number + part_no, 1)
    return block.astype(bf16)


def side_value(block, number):
    return jnp.sum(block.astype(f32) * lane_mask(3 * number, 3), axis=-1, keepdims=True)


def z_route(dp_size, tensor_size, sections, step):
    route = []
    for section in (0, 1):
        for place in range(dp_size):
            other = place ^ (2 * step) if section in sections else place ^ 1
            for column in range(tensor_size):
                route.append(
                    (
                        (section * dp_size + place) * tensor_size + column,
                        (section * dp_size + other) * tensor_size + column,
                    )
                )
    return route


def body(tokens, w_in, w_out, cotangent):
    dp_size = lax.axis_size("dp")
    tensor_size = lax.axis_size("tensor")
    z_size = dp_size // 2
    micro, rows_each, own_width = tokens.shape
    rows = micro * rows_each // STREAMS
    half = rows // 2
    z_rows = half // z_size
    t_rows = half // tensor_size
    width = own_width * dp_size
    pair_width = 2 * own_width
    units = w_in.shape[2]
    streams = range(STREAMS)
    first_section = lax.axis_index("section") == 0
    place = lax.axis_index("dp")
    z_place, core = place // 2, place % 2
    t_place = lax.axis_index("tensor")

    def pick(early, later):
        return jnp.where(first_section, early, later)

    def core_swap(block):
        return lax.ppermute(block, "dp", [(i, i ^ 1) for i in range(dp_size)])

    def section_hop(block, source):
        return lax.ppermute(block, "section", [(source, 1 - source)])

    def turn_axis(parts, axis, bit):
        low = lax.index_in_dim(parts, 0, axis)
        high = lax.index_in_dim(parts, 1, axis)
        return jnp.concatenate(
            [jnp.where(bit == 1, high, low), jnp.where(bit == 1, low, high)], axis
        )

    def turn_z(parts):
        return turn_axis(turn_axis(parts, 0, z_place // 2), 1, z_place % 2)

    def arrange(block):
        parts = turn_z(block.reshape(2, 2, tensor_size // 4, 2, t_rows, block.shape[1]))
        parts = turn_axis(parts, 3, core)
        return jnp.concatenate([parts[:, :, :, 0], parts[:, :, :, 1]], 0).reshape(block.shape)

    def arrange_back(block):
        parts = block.reshape(2, 2, 2, tensor_size // 4, t_rows, block.shape[1])
        parts = turn_axis(parts, 0, core)
        return turn_z(jnp.stack([parts[0], parts[1]], 3)).reshape(block.shape)

    def z_blocks(blocks, sections):
        return [blocks[0]] + [
            lax.ppermute(
                blocks[step], EVERYWHERE, z_route(dp_size, tensor_size, sections, step)
            )
            for step in range(1, z_size)
        ]

    def z_scatter(block, sections):
        return z_blocks([block[k * z_rows : (k + 1) * z_rows] for k in range(z_size)], sections)

    def z_gather(block, sections):
        return jnp.concatenate(z_blocks([block] * z_size, sections), 0)

    def t_scatter(block, *ready):
        block, *ready = lax.optimization_barrier((block, *ready))
        blocks = block.reshape(tensor_size, t_rows, block.shape[1])
        parts = lax.all_to_all(blocks, "tensor", 0, 0)
        return jnp.sum(parts.astype(f32), 0), *ready

    def t_gather(block):
        copies = jnp.broadcast_to(block[None], (tensor_size,) + block.shape)
        return lax.all_to_all(copies, "tensor", 0, 0)

    def t_slab(block):
        return lax.dynamic_slice_in_dim(block, t_place * t_rows, t_rows, 0)

    def own_columns(block):
        return jnp.concatenate([block[:, :own_width], core_swap(block[:, own_width:])], 0)

    def forward_partial(block):
        values = block.astype(f32)
        total = jnp.sum(values, 1, keepdims=True)
        squares = jnp.sum(values * values, 1, keepdims=True)
        product = matmul(block, w_in_pair) - (total / pair_width) * column_sum
        return jnp.concatenate([product.astype(bf16), pack_side([total, squares])], 1)

    def finish_pre(blocks, sums):
        sides = [block[:, units:] for block in blocks]
        totals = [side_value(side, 0) for side in sides]
        squares = sum(side_value(side, 1) for side in sides)
        mean = sum(totals) / width
        inv_scale = lax.rsqrt(squares / width - mean * mean + 1e-05)
        product = sum(block[:, :units].astype(f32) for block in blocks)
        for total, its_sum in zip(totals, sums):
            product = product + (total / pair_width - mean) * its_sum
        return product * inv_scale, mean, inv_scale

    def backward_sums(grad_pre, pre):
        values = grad_pre.astype(f32)
        first = jnp.sum(values * sum(sums), 1, keepdims=True)
        second = jnp.sum(values * pre, 1, keepdims=True)
        return first, second

    def slab_norm(side):
        return side_value(t_slab(side), 0), side_value(t_slab(side), 1)

    def input_gradient(grad_slab, total, input_slab, mean, inv_scale):
        first = side_value(total[:, pair_width:], 2) / width
        second = side_value(total[:, pair_width:], 3) / width
        normed = (input_slab.astype(f32) - mean) * inv_scale
        return (
            grad_slab.astype(f32) + inv_scale * (total[:, :pair_width] - first - normed * second)
        ).astype(bf16)

    with jax.named_scope("tick0"):
        w_in_own, w_out_own = w_in[0], w_out[0]
        w_in_other = core_swap(w_in_own)
        w_in_pair = jnp.concatenate([w_in_own, w_in_other], 0)
        w_out_pair = jnp.concatenate([w_out_own, core_swap(w_out_own)], 1)
        w_in_pair = lax.optimization_barrier(w_in_pair)
        w_out_pair = lax.optimization_barrier(w_out_pair)
        column_sum = matmul(jnp.ones((16, pair_width), bf16), w_in_pair)[:1]
        sum_rows = jnp.concatenate(
            list(three_parts(column_sum)) + [jnp.zeros((13, units), f32)], 0
        ).astype(bf16)
        sum_rows = jnp.concatenate([sum_rows, jnp.zeros((16, LANES), bf16)], 1)
        arriving = pick(tokens, cotangent).reshape(STREAMS, rows, own_width)
        in_own = [arrange(arriving[i]) for i in streams]
        in_half = [jnp.concatenate([own[:half], core_swap(own[half:])], 1) for own in in_own]
        in_slab = [t_slab(block) for block in in_half]
        early = []
        for i in streams:
            partial = forward_partial(in_half[i])
            pieces = [partial[k * z_rows : (k + 1) * z_rows] for k in range(z_size)]
            if i == 0:
                pieces = [jnp.concatenate([piece, sum_rows], 0) for piece in pieces]
            early.append(z_blocks(pieces, (0,)))
        sums = [
            jnp.sum(block[z_rows : z_rows + 3, :units].astype(f32), 0, keepdims=True)
            for block in early[0]
        ]
        early[0] = [block[:z_rows] for block in early[0]]
        early_norm = [finish_pre(blocks, sums) for blocks in early]
        sum_tiles = units // LANES
        sum_block = jnp.concatenate(
            [part.reshape(sum_tiles, LANES) for part in three_parts(column_sum)]
            + [jnp.zeros((z_rows - 3 * sum_tiles, LANES), f32)],
            0,
        ).astype(bf16)
        hidden_early, grad_hidden_later = [], []
        for i in streams:
            pre, mean, inv_scale = early_norm[i]
            share = jnp.concatenate(
                [gelu_value(pre).astype(bf16), pack_side([mean, inv_scale])], 1
            )
            grads = matmul_t(in_half[i], w_out_pair).astype(bf16)
            grads = [
                jnp.concatenate([grads[k * z_rows : (k + 1) * z_rows], sum_block], 1)
                for k in range(z_size)
            ]
            blocks = z_blocks([pick(share, block) for block in grads], (0, 1))
            if i == 0:
                sent = [block[: 3 * sum_tiles, units:].astype(f32) for block in blocks]
                sent = [jnp.sum(x.reshape(3, sum_tiles, LANES), 0) for x in sent]
                sums = [pick(a, x.reshape(1, units)) for a, x in zip(sums, sent)]
            hidden_early.append(jnp.concatenate(blocks, 0))
            grad_hidden_later.append(sum(block[:, :units].astype(f32) for block in blocks))
        middle_slab, middle = [], []
        for i in streams:
            branch, in_slab[i] = t_scatter(
                matmul(hidden_early[i][:, :units], w_out_pair).astype(bf16), in_slab[i]
            )
            slab = (in_slab[i].astype(f32) + branch).astype(bf16)
            slab = pick(slab, section_hop(slab, 0))
            slab, w_in_own, w_in_other = lax.optimization_barrier((slab, w_in_own, w_in_other))
            middle_slab.append(slab)
            middle.append(t_gather(slab).reshape(half, pair_width))

    with jax.named_scope("tick1"):
        w_in_pair = lax.optimization_barrier(jnp.concatenate([w_in_own, w_in_other], 0))
        hidden_share, grad_pre_later, turn_slab, turn = [], [], [], []
        for i in streams:
            blocks = z_scatter(forward_partial(middle[i]), (1,))
            pre, mean, inv_scale = finish_pre(blocks, sums)
            hidden_share.append(gelu_value(pre).astype(bf16))
            grad_pre = (grad_hidden_later[i] * gelu_slope(pre)).astype(bf16)
            side = pack_side([mean, inv_scale, *backward_sums(grad_pre, pre)])
            grad_pre_later.append(z_gather(jnp.concatenate([grad_pre, side], 1), (1,)))
        for i in streams:
            side = grad_pre_later[i][:, units:]
            partial = matmul_t(grad_pre_later[i][:, :units], w_in_pair).astype(bf16)
            total, *norm = t_scatter(jnp.concatenate([partial, side], 1), *slab_norm(side))
            slab = input_gradient(in_slab[i], total, middle_slab[i], *norm)
            slab = pick(section_hop(slab, 1), slab)
            turn_slab.append(slab)
            turn.append(t_gather(slab).reshape(half, pair_width))

    with jax.named_scope("tick2"):
        last, totals, last_norm = [], [], []
        for i in streams:
            blocks = z_scatter(matmul_t(turn[i], w_out_pair).astype(bf16), (0,))
            grad_hidden = sum(block.astype(f32) for block in blocks)
            pre, mean, inv_scale = early_norm[i]
            grad_pre = (grad_hidden * gelu_slope(pre)).astype(bf16)
            side = pack_side([mean, inv_scale, *backward_sums(grad_pre, pre)])
            share = jnp.concatenate([pick(grad_pre, hidden_share[i]), side], 1)
            last.append(z_gather(share, (0, 1)))
        for i in streams:
            partial = pick(
                matmul_t(last[i][:, :units], w_in_pair), matmul(last[i][:, :units], w_out_pair)
            ).astype(bf16)
            side = last[i][:, units:]
            total, *norm = t_scatter(jnp.concatenate([partial, side], 1), *slab_norm(side))
            totals.append(total)
            last_norm.append(norm)

    with jax.named_scope("weights"):
        middle_own = [own_columns(block) for block in middle]
        turn_own = [own_columns(block) for block in turn]

        def both_halves(early_halves, later_halves):
            halves = [pick(*pair) for pair in zip(early_halves, later_halves)]
            return jnp.concatenate([x for h in halves for x in (h, core_swap(h))], 0)

        grad_pre_all = both_halves(last, grad_pre_later)
        hidden_all = both_halves(hidden_early, last)
        side = grad_pre_all[:, units:]
        own_input = jnp.concatenate(in_own, 0)
        section_input = pick(own_input, jnp.concatenate(middle_own, 0)).astype(f32)
        normed = ((section_input - side_value(side, 0)) * side_value(side, 1)).astype(bf16)
        grad_out = pick(jnp.concatenate(turn_own, 0), own_input)
        grad_w_out = matmul_ta(hidden_all[:, :units], grad_out).astype(bf16)
        grad_w_in = matmul_ta(normed, grad_pre_all[:, :units]).astype(bf16)

    with jax.named_scope("last"):
        totals[-1], grad_w_out, normed = lax.optimization_barrier((totals[-1], grad_w_out, normed))
        final = []
        for i in streams:
            slab = pick(
                input_gradient(turn_slab[i], totals[i], in_slab[i], *last_norm[i]),
                (middle_slab[i].astype(f32) + totals[i][:, :pair_width]).astype(bf16),
            )
            pair = turn_axis(own_columns(slab).reshape(2, t_rows, own_width), 0, core)
            final.append(t_gather(pair))
        final[-1], grad_w_in = lax.optimization_barrier((final[-1], grad_w_in))
        final = [
            turn_z(x.reshape(2, 2, tensor_size // 4, 2, t_rows, own_width)).reshape(rows, own_width)
            for x in final
        ]

    shape = (1,) + tokens.shape
    middle_out = jnp.concatenate([arrange_back(block) for block in middle_own], 0)
    turn_out = jnp.concatenate([arrange_back(block) for block in turn_own], 0)
    final_out = jnp.concatenate(final, 0)
    return (
        pick(middle_out, final_out).reshape(shape),
        pick(final_out, turn_out).reshape(shape),
        grad_w_in[None],
        grad_w_out[None],
    )


def solution(mesh):
    in_specs = (
        P(None, None, "dp"),
        P("section", "dp", "tensor"),
        P("section", "tensor", "dp"),
        P(None, None, "dp"),
    )
    out_specs = (
        P("section", None, None, "dp"),
        P("section", None, None, "dp"),
        P("section", "dp", "tensor"),
        P("section", "tensor", "dp"),
    )
    return jax.shard_map(body, mesh=mesh, in_specs=in_specs, out_specs=out_specs, check_vma=False)
```
